32 devices in a mesh: groups: 2 (over x), chan: 16 (over z, y, core).
Axes of the slice: x: 2, y: 2, z: 4, core: 2. Of those that a mesh axis runs over, the one named last changes fastest.
Arguments:
- traces: float32 [1024, 4, 2048], P(('groups', 'chan')), parts along dimension 0, may hold values from -60 to 60
- fir_taps: float32 [32], replicated, may hold values from -1 to 1
- pair_list: int32 [64, 4, 256], P('groups'), parts along dimension 0, may hold values from 0 to 32767, as said below
- owners: int32 [64, 1], P('groups'), parts along dimension 0, may hold values from 0 to 15; in each aligned block of 32 rows (0 to 31, 32 to 63, ...) at most 8 rows name the same one
Outputs:
- gathers: float32 [256, 4, 256], P(('groups', 'chan')), parts along dimension 0
The draws below stay inside these ranges and needn't reach their ends.
There are 2 independent parts, one for each index of `groups`. The reference program is written for one: setup_inputs(seed, part) draws one part's arguments, and reference() takes and returns one part's arrays. A program takes and returns all parts, laid end to end along the dimension named above; an argument that names none is the same for every part. Nothing has to cross between parts.
Inputs may be any that keep to these rules, and one draw needn't show every extreme that they name: `pair_list`: every pair id appears exactly once in the list. `owners`: no owner holds more than 8 virtual sources, some owner holds exactly 8, and every block owns at least one.
All inputs are finite; a program needn't handle non-finite values.
Results may differ from the reference program's by a relative error of at most 0.0033.
Values may be sent and summed in bfloat16 or wider, within the bound.
A program may use at most 64 MiB of HBM per device.

```python
import math
import jax
import jax.numpy as jnp
import numpy as np
from jax import lax

CH_DEV = 32
NWIN = 4
WLEN = 2048
LAGS = 256
TAPS = 32
RCV = 4
K = 256
CHANNELS = 512
NSRC = 32
CAP = 8
TOTAL_PAIRS = 32768
N_CHAN = 16


def draw_traces(key, part):
    key = jax.random.fold_in(key, 11)
    noise_key, level_key = jax.random.split(key)
    segment_count = WLEN // 64
    noise_draw = jnp.clip(jax.random.normal(noise_key, (CHANNELS, NWIN, WLEN), jnp.float32), -4.0, 4.0)
    upper_log = math.log(10.0)
    levels = jnp.exp(jax.random.uniform(level_key, (CHANNELS, NWIN, segment_count), jnp.float32, 0.0, upper_log))
    envelope = jnp.repeat(levels, 64, axis=2)
    return noise_draw * envelope


def draw_pair_list(key, part):
    key = jax.random.fold_in(key, 23)
    order = jax.random.permutation(key, TOTAL_PAIRS).astype(jnp.int32)
    return order.reshape(NSRC, RCV, K)


def assign_block(rng, own, number, rows, count, top, most, lean):
    ranking = jax.random.permutation(rng, count)
    crowded, common = load_shares(count, rows * top, most, lean, True), load_shares(count, rows * top, most, lean, False)
    places = jnp.arange(count)

    def named(lengths, offset_by):
        used = int((lengths > 0).sum())
        fixed = max(1, used // 4)
        passed = fixed + (places - fixed + offset_by * (used - fixed)) % max(1, count - fixed)
        return jnp.zeros((count,), jnp.int32).at[ranking[jnp.where(places < fixed, places, passed)]].set(jnp.asarray(lengths, jnp.int32))

    lengths = jnp.where(number % 4 == 0, named(crowded, number // 4), named(common, number - number // 4 - 1))
    mixed = jax.random.permutation(jax.random.fold_in(own, 3), count)
    source_of, sink = mixed[0:count // 2 * 2:2], mixed[1:count // 2 * 2:2]
    room = jnp.minimum(lengths[source_of] - 1, most - lengths[sink]) // 2
    room = jnp.where((source_of == ranking[0]) | (sink == ranking[0]) | (lengths[sink] == 0), 0, jnp.maximum(room, 0))
    passed = jax.random.randint(jax.random.fold_in(own, 4), (count // 2,), 0, 1 << 20) % (room + 1)
    lengths = lengths.at[source_of].add(-passed).at[sink].add(passed)
    items = jnp.searchsorted(jnp.cumsum(lengths), jnp.arange(rows * top), side="right").astype(jnp.int32)
    table = items.reshape(top, rows).T
    table = table[jax.random.permutation(jax.random.fold_in(own, 1), rows)]
    offset_by = jax.random.randint(jax.random.fold_in(own, 2), (rows, 1), 0, top)
    return jnp.take_along_axis(table, (jnp.arange(top)[None, :] + offset_by) % top, axis=1)


def load_shares(amount, total, limit, slope, full):
    weights = [(1 << 20) // math.isqrt(standing ** slope) + 1 for standing in range(1, amount + 1)]
    largest = limit if full else min(limit, max(-(-total // amount), total * weights[0] // sum(weights)))
    least = 1 if total - largest >= amount - 1 else 0
    holding, surplus = [largest] + [least] * (amount - 1), total - largest - least * (amount - 1)
    while surplus > 0:
        free = [i for i in range(1, amount) if holding[i] < largest] or [i for i in range(1, amount) if holding[i] < limit]
        pool, left = sum([weights[i] for i in free]), surplus
        for i in free:
            addition = min(limit - holding[i], max(1, left * weights[i] // pool), surplus)
            holding[i] = holding[i] + addition
            surplus = surplus - addition
    return np.array(holding)


def bell_draw(rng, shape, spread, reach, held_as=jnp.bfloat16):
    entries = jax.random.normal(rng, shape, jnp.float32) * spread
    return jnp.minimum(jnp.maximum(entries, -reach), reach).astype(held_as)


def setup_inputs(seed: int = 0, part: int = 0) -> dict:
    key_list = jax.random.split(jax.random.key(seed), 5)
    part_keys = jax.random.split(jax.random.fold_in(key_list[4], part), 5)
    traces = draw_traces(jax.random.fold_in(jax.random.fold_in(key_list[4], part), 71), part)
    fir_taps = bell_draw(key_list[1], (TAPS,), TAPS ** -0.5, 1.0, jnp.float32)
    pair_list = draw_pair_list(jax.random.fold_in(jax.random.fold_in(key_list[4], part), 71), part)
    owners_keys = jax.random.split(jax.random.fold_in(part_keys[3], 1), NSRC // NSRC)
    owners_turns = jax.random.permutation(jax.random.fold_in(part_keys[3], 3), NSRC // NSRC)
    owners = jax.vmap(lambda own, number: assign_block(jax.random.fold_in(part_keys[3], 2), own, number, NSRC, N_CHAN, 1, CAP, 2))(owners_keys, owners_turns).reshape((NSRC, 1))
    return dict(traces=traces, fir_taps=fir_taps, pair_list=pair_list, owners=owners)


epsilon = 1e-06

def whiten(traces, fir_taps):
    length = traces.shape[2]
    padded = jnp.pad(traces, ((0, 0), (0, 0), (TAPS - 1, 0)))
    filtered = jnp.zeros(traces.shape, jnp.float32)
    for offset in range(TAPS):
        begin = TAPS - 1 - offset
        filtered = filtered + fir_taps[offset] * padded[:, :, begin:begin + length]
    signal_power = lax.optimization_barrier(jnp.mean(filtered * filtered, axis=2, keepdims=True))
    return (filtered * lax.rsqrt(signal_power + epsilon)).astype(jnp.bfloat16)

def source_slots(owners):
    owner_ids = owners[:, 0]
    positions = jnp.arange(owner_ids.shape[0], dtype=jnp.int32)
    same_owner = owner_ids[:, None] == owner_ids[None, :]
    earlier = positions[None, :] < positions[:, None]
    source_rank = lax.optimization_barrier(jnp.sum((same_owner & earlier).astype(jnp.int32), axis=1))
    return owner_ids * CAP + source_rank

def correlate(partner, own_block):
    return lax.conv_general_dilated(partner, own_block, window_strides=(1,), padding=[(0, LAGS - 1)], dimension_numbers=('NCH', 'OIH', 'NCH'), precision=lax.Precision.HIGHEST, preferred_element_type=jnp.float32)

def reference(traces, fir_taps, pair_list, owners):
    white_half = whiten(traces, fir_taps)
    white_full = lax.optimization_barrier(white_half).astype(jnp.float32)
    blocks = white_full.reshape(N_CHAN, CH_DEV, NWIN, WLEN)
    next_blocks = jnp.roll(blocks, -1, axis=0)
    far_blocks = jnp.roll(blocks, -2, axis=0)

    def one_block(block_items):
        own_block, first_block, second_block = block_items
        partners = jnp.concatenate([first_block, second_block], axis=0)
        return correlate(partners, own_block).reshape(2 * CH_DEV * CH_DEV, LAGS)
    pair_table = lax.map(one_block, (blocks, next_blocks, far_blocks)).reshape(TOTAL_PAIRS, LAGS)
    pair_table = pair_table * (1.0 / (NWIN * WLEN) ** 0.5)
    stacked = lax.optimization_barrier(jnp.sum(pair_table[pair_list], axis=2))
    slot_of = source_slots(owners)
    gathers = jnp.zeros((N_CHAN * CAP, RCV, LAGS), jnp.float32).at[slot_of].set(stacked)
    return gathers
```

```python
import jax
import jax.numpy as jnp
from jax import lax
from jax.experimental import pallas as pl
from jax.experimental.pallas import tpu as pltpu
from jax.sharding import PartitionSpec as P

NWIN = 4
WLEN = 2048
LAGS = 256
TAPS = 32
CAP = 8
PHASES = 8
TILE = 128


epsilon = 1e-06


def shifted(value, axis, by):
    count = lax.axis_size(axis)
    return lax.ppermute(value, axis, [(i, (i + by) % count) for i in range(count)])


def whiten(traces, fir_taps):
    chans, wins, length = traces.shape
    tiles = traces.reshape(chans * wins, length // TILE, TILE)
    before = jnp.pad(tiles, ((0, 0), (1, 0), (0, 0)))[:, :-1]
    stretch = jnp.concatenate([before, tiles], axis=2)
    lag = TILE + jnp.arange(TILE)[None, :] - jnp.arange(2 * TILE)[:, None]
    hot = lag[:, :, None] == jnp.arange(TAPS)[None, None, :]
    band = jnp.sum(jnp.where(hot, fir_taps[None, None, :], 0.0), axis=2)
    filtered = jnp.einsum("rbk,kt->rbt", stretch, band, precision=lax.Precision.HIGHEST)
    signal_power = jnp.mean(filtered * filtered, axis=(1, 2), keepdims=True)
    white = (filtered * lax.rsqrt(signal_power + epsilon)).astype(jnp.bfloat16)
    white = white.reshape(chans, wins, length // PHASES, PHASES)
    return white.transpose(2, 1, 3, 0).reshape(length // PHASES * wins, PHASES * chans)


def correlation_kernel(own_ref, partner_ref, out_ref, product_ref):
    depth, width = own_ref.shape[1], own_ref.shape[0]
    chans = width // PHASES
    norm_factor = 1.0 / (NWIN * WLEN) ** 0.5
    lane = lax.broadcasted_iota(jnp.int32, (chans, width), 1)

    def product(copy, begin):
        rows = partner_ref[0, copy, pl.ds(begin, depth), :]
        return jnp.dot(own_ref[...], rows, preferred_element_type=jnp.float32)

    product_ref[0] = product(0, 0)

    def step(quad, carry):
        for r in range(4):
            d = r + 1
            now, later = r % 2, (r + 1) % 2
            begin = pl.multiple_of((quad + d // 4) * 16, 16)
            product_ref[later] = product(d % 4, begin)
            total = product_ref[now, 0:chans, :]
            for v in range(1, PHASES):
                rows = pl.ds(v * chans, chans)
                mixed = jnp.where(
                    lane < v * chans, product_ref[later, rows, :], product_ref[now, rows, :]
                )
                total = total + pltpu.roll(mixed, width - v * chans, 1)
            out_ref[0, quad * 4 + r] = total * norm_factor
        return carry

    lax.fori_loop(0, LAGS // PHASES // 4, step, 0)


def correlate(own, partners):
    depth, width = own.shape
    steps = LAGS // PHASES
    chans = width // PHASES
    rows = depth + steps * NWIN
    padded = jnp.pad(partners, ((0, 0), (0, rows - depth + 16), (0, 0)))
    copies = jnp.stack([padded[:, 4 * r : 4 * r + rows] for r in range(4)], axis=1)
    return pl.pallas_call(
        correlation_kernel,
        grid=(2,),
        out_shape=jax.ShapeDtypeStruct((2, steps, chans, width), jnp.float32),
        in_specs=[
            pl.BlockSpec((width, depth), lambda s: (0, 0)),
            pl.BlockSpec((1, 4, rows, width), lambda s: (s, 0, 0, 0)),
        ],
        out_specs=pl.BlockSpec((1, steps, chans, width), lambda s: (s, 0, 0, 0)),
        scratch_shapes=[pltpu.VMEM((2, width, width), jnp.float32)],
        compiler_params=pltpu.CompilerParams(vmem_limit_bytes=40 * 2**20),
        cost_estimate=pl.CostEstimate(
            flops=4 * (steps + 1) * width * width * depth, bytes_accessed=8 * 2**20, transcendentals=0
        ),
        name="correlation",
    )(own.T, copies)


def membership_kernel(ids_ref, out_ref):
    bins, per_bin = ids_ref.shape
    high_count, low_count = out_ref.shape[1:]
    high_ids = lax.broadcasted_iota(jnp.int32, (high_count, per_bin), 0)
    low_ids = lax.broadcasted_iota(jnp.int32, (low_count, per_bin), 0)
    for b in range(bins):
        ids = ids_ref[b : b + 1, :]
        high = jnp.where(high_ids == (ids >> 5), 1.0, 0.0).astype(jnp.bfloat16)
        low = jnp.where(low_ids == (ids & 31), 1.0, 0.0).astype(jnp.bfloat16)
        out_ref[b] = lax.dot_general(
            high, low, (((1,), (1,)), ((), ())), preferred_element_type=jnp.float32
        )


def membership(relative, high_count, low_count):
    bins, per_bin = relative.shape
    block = 16
    return pl.pallas_call(
        membership_kernel,
        grid=(bins // block,),
        out_shape=jax.ShapeDtypeStruct((bins, high_count, low_count), jnp.float32),
        in_specs=[pl.BlockSpec((block, per_bin), lambda b: (b, 0))],
        out_specs=pl.BlockSpec((block, high_count, low_count), lambda b: (b, 0, 0)),
        cost_estimate=pl.CostEstimate(
            flops=2 * bins * per_bin * high_count * 128, bytes_accessed=4 * 2**20, transcendentals=0
        ),
        name="membership",
    )(relative)


def source_slots(owners):
    owner_ids = owners[:, 0]
    positions = jnp.arange(owner_ids.shape[0], dtype=jnp.int32)
    same_owner = owner_ids[:, None] == owner_ids[None, :]
    earlier = positions[None, :] < positions[:, None]
    source_rank = jnp.sum((same_owner & earlier).astype(jnp.int32), axis=1)
    return owner_ids * CAP + source_rank


def local(traces, fir_taps, pair_list, owners):
    device_index = lax.axis_index("chan")
    chans = traces.shape[0]
    own = whiten(traces, fir_taps)
    partners = jnp.stack([shifted(own, "chan", -1), shifted(own, "chan", -2)])
    corr = correlate(own, partners)
    steps = LAGS // PHASES
    pair_table = corr.reshape(2, steps, chans, PHASES, chans).transpose(0, 4, 2, 1, 3)
    pairs_here = 2 * chans * chans
    pair_table = pair_table.reshape(pairs_here, LAGS)
    source_count, bin_width, per_bin = pair_list.shape
    relative = pair_list.reshape(source_count * bin_width, per_bin) - device_index * pairs_here
    onehot = membership(relative, 2 * chans, chans).reshape(source_count * bin_width, pairs_here)
    stacked = jnp.dot(
        onehot, pair_table, precision=lax.Precision.HIGHEST, preferred_element_type=jnp.float32
    )
    slot_of = source_slots(owners)
    wanted = jnp.arange(lax.axis_size("chan") * CAP, dtype=jnp.int32)
    select = (slot_of[None, :] == wanted[:, None]).astype(jnp.float32)
    placed = jnp.dot(
        select, stacked.reshape(source_count, bin_width * LAGS), precision=lax.Precision.HIGHEST
    ).reshape(-1, bin_width, LAGS)
    return lax.psum_scatter(placed, "chan", scatter_dimension=0, tiled=True)


def solution(mesh):
    in_specs = (P(("groups", "chan"), None, None), P(), P("groups", None, None), P("groups", None))
    out_specs = P(("groups", "chan"), None, None)
    return jax.shard_map(local, mesh=mesh, in_specs=in_specs, out_specs=out_specs, check_vma=False)
```

```python
import jax
import jax.numpy as jnp
from jax import lax
from jax.experimental import pallas as pl
from jax.experimental.pallas import tpu as pltpu
from jax.sharding import PartitionSpec as P

NWIN = 4
WLEN = 2048
LAGS = 256
TAPS = 32
CAP = 8
PHASES = 8
TILE = 128


epsilon = 1e-06


def shifted(value, axis, by):
    count = lax.axis_size(axis)
    return lax.ppermute(value, axis, [(i, (i + by) % count) for i in range(count)])


def whiten_kernel(traces_ref, band_ref, out_ref, filtered_ref):
    tiles, _, rows = filtered_ref.shape
    chans = rows // NWIN
    ticks = TILE // PHASES
    power = jnp.zeros((1, rows), jnp.float32)
    for b in range(tiles):
        block = lax.dot_general(
            band_ref[...],
            traces_ref[:, b * TILE : (b + 2) * TILE],
            (((1,), (1,)), ((), ())),
            precision=lax.Precision.HIGHEST,
            preferred_element_type=jnp.float32,
        )
        filtered_ref[b] = block
        power = power + jnp.sum(block * block, axis=0, keepdims=True)
    scale = lax.rsqrt(power * (1.0 / WLEN) + epsilon)
    lane = lax.broadcasted_iota(jnp.int32, (ticks, rows), 1) // chans

    def place(b, carry):
        pieces = [filtered_ref[b, v * ticks : (v + 1) * ticks, :] * scale for v in range(PHASES)]
        begin = pl.multiple_of(b * ticks, ticks)
        for w in range(NWIN):
            for half in range(PHASES // NWIN):
                total = jnp.zeros((ticks, rows), jnp.float32)
                for c in range(NWIN):
                    piece = pieces[half * NWIN + c]
                    by = (c - w) * chans % rows
                    moved = pltpu.roll(piece, by, 1) if by else piece
                    total = jnp.where(lane == c, moved, total)
                out_ref[w, pl.ds(begin, ticks), half * rows : (half + 1) * rows] = total.astype(
                    jnp.bfloat16
                )
        return carry

    lax.fori_loop(0, tiles, place, 0)


def whiten(traces, fir_taps):
    chans, wins, length = traces.shape
    rows = chans * wins
    ordered = jnp.pad(traces.transpose(1, 0, 2).reshape(rows, length), ((0, 0), (TILE, 0)))
    line = jnp.arange(TILE)
    ticks = TILE // PHASES
    when = (line % ticks) * PHASES + line // ticks
    lag = TILE + when[:, None] - jnp.arange(2 * TILE)[None, :]
    hot = lag[:, :, None] == jnp.arange(TAPS)[None, None, :]
    band = jnp.sum(jnp.where(hot, fir_taps[None, None, :], 0.0), axis=2)
    white = pl.pallas_call(
        whiten_kernel,
        out_shape=jax.ShapeDtypeStruct((wins, length // PHASES, PHASES * chans), jnp.bfloat16),
        in_specs=[pl.BlockSpec(memory_space=pltpu.VMEM)] * 2,
        out_specs=pl.BlockSpec(memory_space=pltpu.VMEM),
        scratch_shapes=[pltpu.VMEM((length // TILE, TILE, rows), jnp.float32)],
        compiler_params=pltpu.CompilerParams(vmem_limit_bytes=16 * 2**20),
        name="whitening",
    )(ordered, band)
    return white.transpose(1, 0, 2).reshape(length // PHASES * wins, PHASES * chans)


def exchange_kernel(placed_ref, out_ref, arrived, send_sems, recv_sems):
    count, rows = placed_ref.shape[:2]
    me = lax.axis_index("chan")
    barrier = pltpu.get_barrier_semaphore()
    for k in range(1, count):
        pl.semaphore_signal(
            barrier, inc=1, device_id={"chan": lax.rem(me + k, count)}, device_id_type=pl.DeviceIdType.MESH
        )
    pl.semaphore_wait(barrier, count - 1)
    copies = []
    for k in range(1, count):
        peer = lax.rem(me + k, count)
        copy = pltpu.make_async_remote_copy(
            src_ref=placed_ref.at[peer],
            dst_ref=arrived.at[k],
            send_sem=send_sems.at[k],
            recv_sem=recv_sems.at[k],
            device_id={"chan": peer},
            device_id_type=pl.DeviceIdType.MESH,
        )
        copy.start()
        copies.append(copy)
    total = placed_ref[me]
    for k, copy in enumerate(copies, 1):
        copy.wait_recv()
        total = total + arrived[k]
    out_ref[...] = total
    for copy in copies:
        copy.wait_send()


def exchange(placed):
    count, rows, width = placed.shape
    return pl.pallas_call(
        exchange_kernel,
        out_shape=jax.ShapeDtypeStruct((rows, width), jnp.float32),
        in_specs=[pl.BlockSpec(memory_space=pltpu.VMEM)],
        out_specs=pl.BlockSpec(memory_space=pltpu.VMEM),
        scratch_shapes=[
            pltpu.VMEM((count, rows, width), jnp.float32),
            pltpu.SemaphoreType.DMA((count,)),
            pltpu.SemaphoreType.DMA((count,)),
        ],
        compiler_params=pltpu.CompilerParams(
            collective_id=0, has_side_effects=True, vmem_limit_bytes=16 * 2**20
        ),
        name="exchange",
    )(placed)


def correlation_kernel(own_ref, partner_ref, out_ref, product_ref):
    depth, width = own_ref.shape[1], own_ref.shape[0]
    chans = width // PHASES
    norm_factor = 1.0 / (NWIN * WLEN) ** 0.5
    lane = lax.broadcasted_iota(jnp.int32, (chans, width), 1)

    def product(copy, begin):
        rows = partner_ref[0, copy, pl.ds(begin, depth), :]
        return jnp.dot(own_ref[...], rows, preferred_element_type=jnp.float32)

    product_ref[0] = product(0, 0)

    def step(quad, carry):
        for r in range(4):
            d = r + 1
            now, later = r % 2, (r + 1) % 2
            begin = pl.multiple_of((quad + d // 4) * 16, 16)
            product_ref[later] = product(d % 4, begin)
            total = product_ref[now, 0:chans, :]
            for v in range(1, PHASES):
                rows = pl.ds(v * chans, chans)
                mixed = jnp.where(
                    lane < v * chans, product_ref[later, rows, :], product_ref[now, rows, :]
                )
                total = total + pltpu.roll(mixed, width - v * chans, 1)
            out_ref[0, quad * 4 + r] = total * norm_factor
        return carry

    lax.fori_loop(0, LAGS // PHASES // 4, step, 0)


def correlate(own, partners):
    depth, width = own.shape
    steps = LAGS // PHASES
    chans = width // PHASES
    rows = depth + steps * NWIN
    padded = jnp.pad(partners, ((0, 0), (0, rows - depth + 16), (0, 0)))
    copies = jnp.stack([padded[:, 4 * r : 4 * r + rows] for r in range(4)], axis=1)
    return pl.pallas_call(
        correlation_kernel,
        grid=(2,),
        out_shape=jax.ShapeDtypeStruct((2, steps, chans, width), jnp.float32),
        in_specs=[
            pl.BlockSpec((width, depth), lambda s: (0, 0)),
            pl.BlockSpec((1, 4, rows, width), lambda s: (s, 0, 0, 0)),
        ],
        out_specs=pl.BlockSpec((1, steps, chans, width), lambda s: (s, 0, 0, 0)),
        scratch_shapes=[pltpu.VMEM((2, width, width), jnp.float32)],
        compiler_params=pltpu.CompilerParams(vmem_limit_bytes=40 * 2**20),
        cost_estimate=pl.CostEstimate(
            flops=4 * (steps + 1) * width * width * depth, bytes_accessed=8 * 2**20, transcendentals=0
        ),
        name="correlation",
    )(own.T, copies)


def membership_kernel(ids_ref, out_ref):
    bins, per_bin = ids_ref.shape
    high_count, low_count = out_ref.shape[1:]
    high_ids = lax.broadcasted_iota(jnp.int32, (high_count, per_bin), 0)
    low_ids = lax.broadcasted_iota(jnp.int32, (low_count, per_bin), 0)
    for b in range(bins):
        ids = ids_ref[b : b + 1, :]
        high = jnp.where(high_ids == (ids >> 5), 1.0, 0.0).astype(jnp.bfloat16)
        low = jnp.where(low_ids == (ids & 31), 1.0, 0.0).astype(jnp.bfloat16)
        out_ref[b] = lax.dot_general(
            high, low, (((1,), (1,)), ((), ())), preferred_element_type=jnp.float32
        )


def membership(relative, high_count, low_count):
    bins, per_bin = relative.shape
    block = 16
    return pl.pallas_call(
        membership_kernel,
        grid=(bins // block,),
        out_shape=jax.ShapeDtypeStruct((bins, high_count, low_count), jnp.float32),
        in_specs=[pl.BlockSpec((block, per_bin), lambda b: (b, 0))],
        out_specs=pl.BlockSpec((block, high_count, low_count), lambda b: (b, 0, 0)),
        cost_estimate=pl.CostEstimate(
            flops=2 * bins * per_bin * high_count * 128, bytes_accessed=4 * 2**20, transcendentals=0
        ),
        name="membership",
    )(relative)


def source_slots(owners):
    owner_ids = owners[:, 0]
    positions = jnp.arange(owner_ids.shape[0], dtype=jnp.int32)
    same_owner = owner_ids[:, None] == owner_ids[None, :]
    earlier = positions[None, :] < positions[:, None]
    source_rank = jnp.sum((same_owner & earlier).astype(jnp.int32), axis=1)
    return owner_ids * CAP + source_rank


def local(traces, fir_taps, pair_list, owners):
    device_index = lax.axis_index("chan")
    chans = traces.shape[0]
    own = whiten(traces, fir_taps)
    partners = jnp.stack([shifted(own, "chan", -1), shifted(own, "chan", -2)])
    corr = correlate(own, partners)
    steps = LAGS // PHASES
    pair_table = corr.reshape(2, steps, chans, PHASES, chans).transpose(0, 4, 2, 1, 3)
    pairs_here = 2 * chans * chans
    pair_table = pair_table.reshape(pairs_here, LAGS)
    source_count, bin_width, per_bin = pair_list.shape
    relative = pair_list.reshape(source_count * bin_width, per_bin) - device_index * pairs_here
    onehot = membership(relative, 2 * chans, chans).reshape(source_count * bin_width, pairs_here)
    stacked = jnp.dot(
        onehot, pair_table, precision=lax.Precision.HIGHEST, preferred_element_type=jnp.float32
    )
    slot_of = source_slots(owners)
    wanted = jnp.arange(lax.axis_size("chan") * CAP, dtype=jnp.int32)
    select = (slot_of[None, :] == wanted[:, None]).astype(jnp.float32)
    placed = jnp.dot(
        select, stacked.reshape(source_count, bin_width * LAGS), precision=lax.Precision.HIGHEST
    ).reshape(-1, CAP * bin_width, LAGS)
    return exchange(placed).reshape(CAP, bin_width, LAGS)


def solution(mesh):
    in_specs = (P(("groups", "chan"), None, None), P(), P("groups", None, None), P("groups", None))
    out_specs = P(("groups", "chan"), None, None)
    return jax.shard_map(local, mesh=mesh, in_specs=in_specs, out_specs=out_specs, check_vma=False)
```

```python
import jax
import jax.numpy as jnp
from jax import lax
from jax.experimental import pallas as pl
from jax.experimental.pallas import tpu as pltpu
from jax.sharding import PartitionSpec as P

NWIN = 4
WLEN = 2048
LAGS = 256
TAPS = 32
CAP = 8
PHASES = 8
TILE = 128


epsilon = 1e-06


def shifted(value, axis, by):
    count = lax.axis_size(axis)
    return lax.ppermute(value, axis, [(i, (i + by) % count) for i in range(count)])


def whiten_kernel(traces_ref, band_ref, out_ref, filtered_ref):
    tiles, _, rows = filtered_ref.shape
    chans = rows // NWIN
    ticks = TILE // PHASES
    power = jnp.zeros((1, rows), jnp.float32)
    for b in range(tiles):
        block = lax.dot_general(
            band_ref[...],
            traces_ref[:, b * TILE : (b + 2) * TILE],
            (((1,), (1,)), ((), ())),
            precision=lax.Precision.HIGHEST,
            preferred_element_type=jnp.float32,
        )
        filtered_ref[b] = block
        power = power + jnp.sum(block * block, axis=0, keepdims=True)
    scale = lax.rsqrt(power * (1.0 / WLEN) + epsilon)
    lane = lax.broadcasted_iota(jnp.int32, (ticks, rows), 1) // chans

    def place(b, carry):
        pieces = [filtered_ref[b, v * ticks : (v + 1) * ticks, :] * scale for v in range(PHASES)]
        begin = pl.multiple_of(b * ticks, ticks)
        for w in range(NWIN):
            for half in range(PHASES // NWIN):
                total = jnp.zeros((ticks, rows), jnp.float32)
                for c in range(NWIN):
                    piece = pieces[half * NWIN + c]
                    by = (c - w) * chans % rows
                    moved = pltpu.roll(piece, by, 1) if by else piece
                    total = jnp.where(lane == c, moved, total)
                out_ref[w, pl.ds(begin, ticks), half * rows : (half + 1) * rows] = total.astype(
                    jnp.bfloat16
                )
        return carry

    lax.fori_loop(0, tiles, place, 0)


def whiten(traces, fir_taps):
    chans, wins, length = traces.shape
    rows = chans * wins
    ordered = jnp.pad(traces.transpose(1, 0, 2).reshape(rows, length), ((0, 0), (TILE, 0)))
    line = jnp.arange(TILE)
    ticks = TILE // PHASES
    when = (line % ticks) * PHASES + line // ticks
    lag = TILE + when[:, None] - jnp.arange(2 * TILE)[None, :]
    hot = lag[:, :, None] == jnp.arange(TAPS)[None, None, :]
    band = jnp.sum(jnp.where(hot, fir_taps[None, None, :], 0.0), axis=2)
    white = pl.pallas_call(
        whiten_kernel,
        out_shape=jax.ShapeDtypeStruct((wins, length // PHASES, PHASES * chans), jnp.bfloat16),
        in_specs=[pl.BlockSpec(memory_space=pltpu.VMEM)] * 2,
        out_specs=pl.BlockSpec(memory_space=pltpu.VMEM),
        scratch_shapes=[pltpu.VMEM((length // TILE, TILE, rows), jnp.float32)],
        compiler_params=pltpu.CompilerParams(vmem_limit_bytes=16 * 2**20),
        name="whitening",
    )(ordered, band)
    return white.transpose(1, 0, 2).reshape(length // PHASES * wins, PHASES * chans)


def exchange_kernel(placed_ref, out_ref, arrived, send_sems, recv_sems):
    count, rows = placed_ref.shape[:2]
    me = lax.axis_index("chan")
    barrier = pltpu.get_barrier_semaphore()
    for k in range(1, count):
        pl.semaphore_signal(
            barrier, inc=1, device_id={"chan": lax.rem(me + k, count)}, device_id_type=pl.DeviceIdType.MESH
        )
    pl.semaphore_wait(barrier, count - 1)
    copies = []
    for k in range(1, count):
        peer = lax.rem(me + k, count)
        copy = pltpu.make_async_remote_copy(
            src_ref=placed_ref.at[peer],
            dst_ref=arrived.at[k],
            send_sem=send_sems.at[k],
            recv_sem=recv_sems.at[k],
            device_id={"chan": peer},
            device_id_type=pl.DeviceIdType.MESH,
        )
        copy.start()
        copies.append(copy)
    total = placed_ref[me]
    for k, copy in enumerate(copies, 1):
        copy.wait_recv()
        total = total + arrived[k]
    out_ref[...] = total
    for copy in copies:
        copy.wait_send()


def exchange(placed):
    count, rows, width = placed.shape
    return pl.pallas_call(
        exchange_kernel,
        out_shape=jax.ShapeDtypeStruct((rows, width), jnp.float32),
        in_specs=[pl.BlockSpec(memory_space=pltpu.VMEM)],
        out_specs=pl.BlockSpec(memory_space=pltpu.VMEM),
        scratch_shapes=[
            pltpu.VMEM((count, rows, width), jnp.float32),
            pltpu.SemaphoreType.DMA((count,)),
            pltpu.SemaphoreType.DMA((count,)),
        ],
        compiler_params=pltpu.CompilerParams(
            collective_id=0, has_side_effects=True, vmem_limit_bytes=16 * 2**20
        ),
        name="exchange",
    )(placed)


def correlation_kernel(own_ref, partner_ref, out_ref, product_ref):
    depth, width = own_ref.shape[1], own_ref.shape[0]
    chans = width // PHASES
    norm_factor = 1.0 / (NWIN * WLEN) ** 0.5
    lane = lax.broadcasted_iota(jnp.int32, (chans, width), 1)

    def product(copy, begin):
        rows = partner_ref[0, copy, pl.ds(begin, depth), :]
        return jnp.dot(own_ref[...], rows, preferred_element_type=jnp.float32)

    product_ref[0] = product(0, 0)

    def step(quad, carry):
        for r in range(4):
            d = r + 1
            now, later = r % 2, (r + 1) % 2
            begin = pl.multiple_of((quad + d // 4) * 16, 16)
            product_ref[later] = product(d % 4, begin)
            total = product_ref[now, 0:chans, :]
            for v in range(1, PHASES):
                rows = pl.ds(v * chans, chans)
                mixed = jnp.where(
                    lane < v * chans, product_ref[later, rows, :], product_ref[now, rows, :]
                )
                total = total + pltpu.roll(mixed, width - v * chans, 1)
            out_ref[0, :, quad * 4 + r, :] = total * norm_factor
        return carry

    lax.fori_loop(0, LAGS // PHASES // 4, step, 0)


def correlate(own, partners):
    depth, width = own.shape
    steps = LAGS // PHASES
    chans = width // PHASES
    rows = depth + steps * NWIN
    padded = jnp.pad(partners, ((0, 0), (0, rows - depth + 16), (0, 0)))
    copies = jnp.stack([padded[:, 4 * r : 4 * r + rows] for r in range(4)], axis=1)
    return pl.pallas_call(
        correlation_kernel,
        grid=(2,),
        out_shape=jax.ShapeDtypeStruct((2, chans, steps, width), jnp.float32),
        in_specs=[
            pl.BlockSpec((width, depth), lambda s: (0, 0)),
            pl.BlockSpec((1, 4, rows, width), lambda s: (s, 0, 0, 0)),
        ],
        out_specs=pl.BlockSpec((1, chans, steps, width), lambda s: (s, 0, 0, 0)),
        scratch_shapes=[pltpu.VMEM((2, width, width), jnp.float32)],
        compiler_params=pltpu.CompilerParams(vmem_limit_bytes=40 * 2**20),
        cost_estimate=pl.CostEstimate(
            flops=4 * (steps + 1) * width * width * depth, bytes_accessed=8 * 2**20, transcendentals=0
        ),
        name="correlation",
    )(own.T, copies)


def membership_kernel(ids_ref, out_ref):
    bins, per_bin = ids_ref.shape
    high_count, low_count = out_ref.shape[1:]
    high_ids = lax.broadcasted_iota(jnp.int32, (high_count, per_bin), 0)
    low_ids = lax.broadcasted_iota(jnp.int32, (low_count, per_bin), 0)
    for b in range(bins):
        ids = ids_ref[b : b + 1, :]
        place = (ids & 3) * 16 + (ids >> 10) * 8 + ((ids & 31) >> 2)
        place = jnp.where((ids >= 0) & (ids < high_count * low_count), place, -1)
        high = jnp.where(high_ids == place, 1.0, 0.0).astype(jnp.bfloat16)
        low = jnp.where(low_ids == ((ids >> 5) & 31), 1.0, 0.0).astype(jnp.bfloat16)
        out_ref[b] = lax.dot_general(
            high, low, (((1,), (1,)), ((), ())), preferred_element_type=jnp.float32
        )


def membership(relative, high_count, low_count):
    bins, per_bin = relative.shape
    block = 16
    return pl.pallas_call(
        membership_kernel,
        grid=(bins // block,),
        out_shape=jax.ShapeDtypeStruct((bins, high_count, low_count), jnp.float32),
        in_specs=[pl.BlockSpec((block, per_bin), lambda b: (b, 0))],
        out_specs=pl.BlockSpec((block, high_count, low_count), lambda b: (b, 0, 0)),
        cost_estimate=pl.CostEstimate(
            flops=2 * bins * per_bin * high_count * 128, bytes_accessed=4 * 2**20, transcendentals=0
        ),
        name="membership",
    )(relative)


def source_slots(owners):
    owner_ids = owners[:, 0]
    positions = jnp.arange(owner_ids.shape[0], dtype=jnp.int32)
    same_owner = owner_ids[:, None] == owner_ids[None, :]
    earlier = positions[None, :] < positions[:, None]
    source_rank = jnp.sum((same_owner & earlier).astype(jnp.int32), axis=1)
    return owner_ids * CAP + source_rank


def local(traces, fir_taps, pair_list, owners):
    device_index = lax.axis_index("chan")
    chans = traces.shape[0]
    own = whiten(traces, fir_taps)
    partners = jnp.stack([shifted(own, "chan", -1), shifted(own, "chan", -2)])
    corr = correlate(own, partners)
    steps = LAGS // PHASES
    pairs_here = 2 * chans * chans
    four = TILE // steps
    turned = jnp.swapaxes(corr.reshape(2 * chans // four, TILE, PHASES * chans), 1, 2)
    table = turned.reshape(2 * chans // four, PHASES, chans, TILE).transpose(0, 2, 1, 3)
    table = table.reshape(pairs_here // four, PHASES * TILE)
    source_count, bin_width, per_bin = pair_list.shape
    relative = pair_list.reshape(source_count * bin_width, per_bin) - device_index * pairs_here
    bins = source_count * bin_width
    onehot = membership(relative, 2 * chans, chans).reshape(bins * four, pairs_here // four)
    every = jnp.dot(
        onehot, table, precision=lax.Precision.HIGHEST, preferred_element_type=jnp.float32
    ).reshape(bins, four, PHASES, TILE)
    mine = (jnp.arange(TILE)[None, :] // steps) == jnp.arange(four)[:, None]
    kept = jnp.sum(jnp.where(mine[None, :, None, :], every, 0.0), axis=1)
    stacked = jnp.sum(kept.reshape(bins, PHASES, four, steps), axis=2).transpose(0, 2, 1)
    slot_of = source_slots(owners)
    wanted = jnp.arange(lax.axis_size("chan") * CAP, dtype=jnp.int32)
    select = (slot_of[None, :] == wanted[:, None]).astype(jnp.float32)
    placed = jnp.dot(
        select, stacked.reshape(source_count, bin_width * LAGS), precision=lax.Precision.HIGHEST
    ).reshape(-1, CAP * bin_width, LAGS)
    return exchange(placed).reshape(CAP, bin_width, LAGS)


def solution(mesh):
    in_specs = (P(("groups", "chan"), None, None), P(), P("groups", None, None), P("groups", None))
    out_specs = P(("groups", "chan"), None, None)
    return jax.shard_map(local, mesh=mesh, in_specs=in_specs, out_specs=out_specs, check_vma=False)
```
